512 devices in a mesh: span: 32 (over z_lo, x), stream: 16 (over z_hi, y, core).
Axes of the slice: x: 4, y: 4, z: 16 (z_hi: 2, z_lo: 8; z = z_hi * 8 + z_lo), core: 2. Of those that a mesh axis runs over, the one named last changes fastest.
Arguments:
- divergence: bfloat16 [1536, 512, 256], P('span', 'stream'), may hold values from -6 to 6
- flow_basis: float32 [512, 512], P('stream'), may hold values from -1 to 2
- wall_basis: float32 [256, 256], replicated, may hold values from -1 to 2
- flow_mass: float32 [512], replicated, may hold values from 0.5 to 2
- wall_mass: float32 [256], replicated, may hold values from 0.5 to 2
- flow_eigen: float32 [512], replicated, may hold values from 0.2 to 2
- wall_eigen: float32 [256], replicated, may hold values from 0.2 to 2
Outputs:
- pressure: float32 [1536, 512, 256], P(('span', 'stream'))
The draws below stay inside these ranges and needn't reach their ends.
All inputs are finite; a program needn't handle non-finite values.
Results may differ from the reference program's by a relative error of at most 0.0023.
Values may be sent and summed in bfloat16 or wider, within the bound.
A program may use at most 64 MiB of HBM per device.

```python
import math
import jax
import jax.numpy as jnp
from jax import lax

NY = 256
NZ = 1536
NX = 512


def basis_matrix(noise, order):
    return jnp.eye(order, dtype=jnp.float32) + 0.6 * jnp.clip(noise, -4.0, 4.0) / math.sqrt(order)


def draw_flow_basis(key, part):
    key = jax.random.fold_in(key, 11)
    noise = jax.random.normal(key, (NX, NX), jnp.float32)
    return basis_matrix(noise, NX)


def draw_wall_basis(key, part):
    key = jax.random.fold_in(key, 23)
    noise = jax.random.normal(key, (NY, NY), jnp.float32)
    return basis_matrix(noise, NY)


def shard_levels(stream_key, dims, cuts, smallest, largest):
    factor_of = 1.0
    for axis_at, blocks in cuts:
        heights = jax.random.uniform(jax.random.fold_in(jax.random.fold_in(stream_key, 6), axis_at), (blocks,), jnp.float32, smallest / len(cuts), largest / len(cuts))
        factor_of = factor_of * jnp.repeat(jnp.exp(heights), dims[axis_at] // blocks).reshape((-1,) + (1,) * (len(dims) - 1 - axis_at))
    return factor_of


def bell_draw(own_key, dims, deviation, reach, split=(), held_as=jnp.bfloat16):
    array = jax.random.normal(own_key, dims, jnp.float32) * deviation
    if len(split) > 0:
        array = shard_levels(own_key, dims, split, -0.22, 0.18) * array
    return jnp.clip(array, min=-reach, max=reach).astype(held_as)


def setup_inputs(seed: int = 0) -> dict:
    key_list = jax.random.split(jax.random.key(seed), 8)
    divergence = bell_draw(key_list[0], (NZ, NX, NY), 1.0, 6.0, ((0, 32), (1, 16)))
    flow_basis = draw_flow_basis(jax.random.fold_in(key_list[7], 71), 0)
    wall_basis = draw_wall_basis(jax.random.fold_in(key_list[7], 71), 0)
    flow_mass = jnp.clip(jnp.exp(jax.random.uniform(key_list[3], (NX,), jnp.float32, math.log(0.5), math.log(2.0))), 0.5, 2.0)
    wall_mass = jnp.clip(jnp.exp(jax.random.uniform(key_list[4], (NY,), jnp.float32, math.log(0.5), math.log(2.0))), 0.5, 2.0)
    flow_eigen = jnp.clip(jnp.exp(jax.random.uniform(key_list[5], (NX,), jnp.float32, math.log(0.2), math.log(2.0))), 0.2, 2.0)
    wall_eigen = jnp.clip(jnp.exp(jax.random.uniform(key_list[6], (NY,), jnp.float32, math.log(0.2), math.log(2.0))), 0.2, 2.0)
    return dict(divergence=divergence, flow_basis=flow_basis, wall_basis=wall_basis, flow_mass=flow_mass, wall_mass=wall_mass, flow_eigen=flow_eigen, wall_eigen=wall_eigen)


def fourier_rows(field_ids, length):
    midpoint = length // 2
    wavenum = jnp.where(field_ids <= midpoint, field_ids, field_ids - midpoint)
    planes = jnp.arange(length, dtype=jnp.int32)
    phase = (wavenum[:, None] * planes[None, :]) % length
    angle = phase.astype(jnp.float32) * jnp.float32(2.0 * math.pi / length)
    values = jnp.where((field_ids <= midpoint)[:, None], jnp.cos(angle), -jnp.sin(angle))
    return values.astype(jnp.bfloat16)


def wave_terms(field_ids, length):
    midpoint = length // 2
    wavenum = jnp.where(field_ids <= midpoint, field_ids, field_ids - midpoint).astype(jnp.float32)
    ratio = wavenum / jnp.float32(midpoint)
    return ratio * ratio


def reference(divergence, flow_basis, wall_basis, flow_mass, wall_mass, flow_eigen, wall_eigen):
    highest = lax.Precision.HIGHEST
    field_ids = jnp.arange(NZ, dtype=jnp.int32)
    table = fourier_rows(field_ids, NZ)
    spectral = jnp.dot(table, divergence.reshape(NZ, NX * NY), preferred_element_type=jnp.float32)
    spectral = (spectral * (float(NZ) ** -0.5)).reshape(NZ, NX, NY)
    waves = wave_terms(field_ids, NZ)

    def solve_plane(inputs):
        plane, wave = inputs
        along_wall = jnp.dot(plane * wall_mass[None, :], wall_basis, precision=highest)
        coeff = jnp.dot(flow_basis.T, along_wall * flow_mass[:, None], precision=highest)
        solved = coeff / (flow_eigen[:, None] + wall_eigen[None, :] + wave)
        back = jnp.dot(flow_basis, solved, precision=highest)
        return jnp.dot(back, wall_basis.T, precision=highest)

    return lax.map(solve_plane, (spectral, waves))
```

```python
import functools
import math

import jax
import jax.numpy as jnp
import numpy as np
from jax import lax
from jax.experimental import pallas as pl
from jax.experimental.pallas import tpu as pltpu
from jax.sharding import PartitionSpec as P

NZ, NX, NY = 1536, 512, 256
MESH = pl.DeviceIdType.MESH
CHUNKS = 4
BF, F32 = jnp.bfloat16, jnp.float32


def table_sets():
    planes = np.arange(NZ)
    sets = []
    for g in range(2):
        fields = []
        for d in range(16):
            fields += [48 * d + 24 * g + r for r in range(24)]
            fields += [48 * (16 + d) + 24 * (1 - g) + r for r in range(24)]
        f = np.array(fields)
        k = np.where(f <= NZ // 2, f, f - NZ // 2)
        angle = ((k[:, None] * planes[None, :]) % NZ).astype(np.float32) * np.float32(2.0 * math.pi / NZ)
        sets.append(np.where((f <= NZ // 2)[:, None], np.cos(angle), -np.sin(angle)))
    return np.stack(sets).astype(jnp.bfloat16)


def split(a):
    hi = a.astype(BF)
    return hi, (a - hi.astype(F32)).astype(BF)


def dot(a, b):
    return jnp.dot(a, b, preferred_element_type=F32)


def forward_kernel(
    div, flow, table, fmass, wall, wmass,
    proj, fhi, flo, whi, wlo, thi, tlo,
    tbl, slab, spec, abuf, bbuf, lines, perm, gath, fmthi, fmtlo,
    tsem, rsem1, rsema, rsemb, ssem1, ssema, ssemb, gsem, gssem,
):
    s, t = lax.axis_index("span"), lax.axis_index("stream")
    h, d = s // 16, s % 16
    zh, u = t // 8, t % 8
    g = lax.rem(h + zh, 2)

    def span_peer(k):
        other = k // 16
        return lax.rem(h + 1 + other, 2) * 16 + lax.rem(d + k, 16)

    def stream_peer(k):
        own = k // 8
        sp = lax.rem(h + 1 + own, 2) * 16 + d
        tp = lax.rem(zh + 1 + own, 2) * 8 + lax.rem(u + k, 8)
        return sp, tp

    tcopy = pltpu.make_async_copy(table.at[g], tbl, tsem)
    tcopy.start()

    barrier = pltpu.get_barrier_semaphore()

    def greet_span(k, _):
        pl.semaphore_signal(barrier, inc=1, device_id=(span_peer(k), t), device_id_type=MESH)
        return 0

    def greet_stream(k, _):
        pl.semaphore_signal(barrier, inc=1, device_id=stream_peer(k), device_id_type=MESH)
        return 0

    lax.fori_loop(0, 16, greet_span, 0)
    lax.fori_loop(17, 32, greet_span, 0)
    lax.fori_loop(0, 8, greet_stream, 0)
    lax.fori_loop(9, 16, greet_stream, 0)
    pl.semaphore_wait(barrier, 46)

    own_rows = gath.at[pl.ds(pl.multiple_of(t * 32, 32), 32), :]
    pltpu.make_async_copy(flow, own_rows, gsem.at[0]).start()
    pltpu.make_async_remote_copy(
        src_ref=flow, dst_ref=own_rows, send_sem=gssem, recv_sem=gsem.at[1],
        device_id=((1 - h) * 16 + d, (1 - zh) * 8 + u), device_id_type=MESH,
    ).start()

    def share_flow(k, _):
        pltpu.make_async_remote_copy(
            src_ref=flow, dst_ref=own_rows, send_sem=gssem, recv_sem=gsem.at[0],
            device_id=stream_peer(k), device_id_type=MESH,
        ).start()
        return 0

    lax.fori_loop(9, 16, share_flow, 0)

    def send1(c):
        rows = slab.at[c, pl.ds(pl.multiple_of(s * 48, 48), 48), :]

        def one(k, _):
            dst = span_peer(k)
            pltpu.make_async_remote_copy(
                src_ref=div.at[lax.rem(dst, 16), c], dst_ref=rows, send_sem=ssem1.at[c], recv_sem=rsem1.at[c],
                device_id=(dst, t), device_id_type=MESH,
            ).start()
            return 0

        pltpu.make_async_copy(div.at[d, c], rows, rsem1.at[c]).start()
        lax.fori_loop(0, 16, one, 0)
        lax.fori_loop(17, 32, one, 0)

    def wait1(c):
        pltpu.make_async_copy(slab.at[c], slab.at[c], rsem1.at[c]).wait()

    def transform(c):
        def tile(i, _):
            rows = pl.ds(pl.multiple_of(i * 256, 256), 256)
            r = dot(tbl[rows, :], slab[c]) * F32(float(NZ) ** -0.5)
            spec[c, rows, :] = r.astype(BF)
            return 0

        lax.fori_loop(0, 3, tile, 0)

    def senda(c):
        def one(k, _):
            dd = lax.rem(d + k, 16)
            pltpu.make_async_remote_copy(
                src_ref=spec.at[c, pl.ds(pl.multiple_of(dd * 48, 48), 48), :], dst_ref=abuf.at[c, d],
                send_sem=ssema.at[c], recv_sem=rsema.at[c],
                device_id=(h * 16 + dd, t), device_id_type=MESH,
            ).start()
            return 0

        pltpu.make_async_copy(spec.at[c, pl.ds(pl.multiple_of(d * 48, 48), 48), :], abuf.at[c, d], rsema.at[c]).start()
        lax.fori_loop(1, 16, one, 0)

    def waita(c):
        pltpu.make_async_copy(abuf.at[c], abuf.at[c], rsema.at[c]).wait()

    def turn(c):
        def tile(i, _):
            rows = pl.ds(pl.multiple_of(i * 256, 256), 256)
            r = dot(perm[rows, :], abuf[c].reshape(768, 128))
            bbuf[c, pl.ds(pl.multiple_of(i * 16, 16), 16)] = r.reshape(16, 16, 128).astype(BF)
            return 0

        lax.fori_loop(0, 3, tile, 0)

    def sendb(c):
        dst_ref = lines.at[c, :, pl.ds(pl.multiple_of(t * 16, 16), 16), :]

        def one(k, _):
            sp, tp = stream_peer(k)
            pltpu.make_async_remote_copy(
                src_ref=bbuf.at[c, pl.ds((sp // 16) * 24 + lax.rem(tp, 8) * 3, 3)], dst_ref=dst_ref,
                send_sem=ssemb.at[c], recv_sem=rsemb.at[c],
                device_id=(sp, tp), device_id_type=MESH,
            ).start()
            return 0

        lax.fori_loop(0, 8, one, 0)
        pltpu.make_async_copy(bbuf.at[c, pl.ds(h * 24 + u * 3, 3)], dst_ref, rsemb.at[c]).start()
        lax.fori_loop(9, 16, one, 0)

    def waitb(c):
        pltpu.make_async_copy(lines.at[c], lines.at[c], rsemb.at[c]).wait()

    def project(c):
        xp, yh = c // 2, c % 2

        def field(f, _):
            part = dot(fmthi[xp], lines[c, f]) + dot(fmtlo[xp], lines[c, f])
            cols = pl.ds(yh * 128, 128)
            if xp == 0:
                proj[f, :, cols] = part
            else:
                proj[f, :, cols] += part
            return 0

        lax.fori_loop(0, 3, field, 0)

    send1(0)
    send1(1)

    i0 = lax.broadcasted_iota(jnp.int32, (768, 768), 0)
    i1 = lax.broadcasted_iota(jnp.int32, (768, 768), 1)
    perm[...] = jnp.where(lax.rem(i0, 16) * 48 + i0 // 16 == i1, 1.0, 0.0).astype(BF)

    w = wall[...]
    thi[...], tlo[...] = split(w.T)
    wm = jnp.broadcast_to(wmass[...], (128, NY)).T
    for j in range(NY // 128):
        cols = slice(j * 128, (j + 1) * 128)
        whi[:, cols], wlo[:, cols] = split(w[:, cols] * wm)

    far = (1 - zh) * 8 + u
    far_rows = gath.at[pl.ds(pl.multiple_of(far * 32, 32), 32), :]
    pltpu.make_async_copy(far_rows, far_rows, gsem.at[1]).wait()

    def pass_on(k, _):
        pltpu.make_async_remote_copy(
            src_ref=far_rows, dst_ref=far_rows, send_sem=gssem, recv_sem=gsem.at[2],
            device_id=stream_peer(k), device_id_type=MESH,
        ).start()
        return 0

    lax.fori_loop(9, 16, pass_on, 0)
    near = gath.at[pl.ds(0, 256), :]
    pltpu.make_async_copy(near, near, gsem.at[0]).wait()
    rest = gath.at[pl.ds(0, 224), :]
    pltpu.make_async_copy(rest, rest, gsem.at[2]).wait()

    fhi[...], flo[...] = split(gath[...])
    fm = jnp.broadcast_to(fmass[...], (128, NX)).T
    for j in range(NX // 128):
        cols = slice(j * 128, (j + 1) * 128)
        scaled = (gath[:, cols] * fm).reshape(16, 2, 16, 128)
        for xp in range(2):
            fmthi[xp, cols, :], fmtlo[xp, cols, :] = split(scaled[:, xp].reshape(256, 128).T)

    tcopy.wait()
    for c in range(CHUNKS + 2):
        if c < CHUNKS:
            wait1(c)
            transform(c)
            senda(c)
            if c + 2 < CHUNKS:
                send1(c + 2)
        if 1 <= c <= CHUNKS:
            waita(c - 1)
            turn(c - 1)
            sendb(c - 1)
        if c >= 2:
            waitb(c - 2)
            project(c - 2)

    sent = gath.at[pl.ds(0, 480), :]
    pltpu.make_async_copy(sent, sent, gssem).wait()
    for c in range(CHUNKS):
        r1 = slab.at[c, pl.ds(0, 31 * 48), :]
        pltpu.make_async_copy(r1, r1, ssem1.at[c]).wait()
        ra = spec.at[c, pl.ds(0, 15 * 48), :]
        pltpu.make_async_copy(ra, ra, ssema.at[c]).wait()
        rb = bbuf.at[c, pl.ds(0, 45)]
        pltpu.make_async_copy(rb, rb, ssemb.at[c]).wait()


def solve_kernel(proj, fhi, flo, whi, wlo, thi, tlo, feig, weig, out):
    s, t = lax.axis_index("span"), lax.axis_index("stream")
    f = s * 48 + t * 3 + pl.program_id(0)
    k = jnp.where(f <= NZ // 2, f, f - NZ // 2).astype(F32) / F32(NZ // 2)
    ahi, alo = split(proj[0])
    coeff = dot(ahi, whi[...]) + (dot(ahi, wlo[...]) + dot(alo, whi[...]))
    fe = jnp.broadcast_to(feig[...], (128, NX)).T
    denom = jnp.concatenate([fe, fe], axis=1) + weig[...] + k * k
    shi, slo = split(coeff / denom)
    back = dot(fhi[...], shi) + (dot(fhi[...], slo) + dot(flo[...], shi))
    bhi, blo = split(back)
    out[0] = dot(bhi, thi[...]) + (dot(bhi, tlo[...]) + dot(blo, thi[...]))


def local(divergence, flow_basis, wall_basis, flow_mass, wall_mass, flow_eigen, wall_eigen):
    blocks = divergence.reshape(48, 2, 16, 2, 128).transpose(2, 1, 3, 0, 4).reshape(16, CHUNKS, 48, 128)
    table = jnp.asarray(table_sets())
    vmem = pl.BlockSpec(memory_space=pltpu.VMEM)
    hbm = pl.BlockSpec(memory_space=pl.ANY)
    sds = jax.ShapeDtypeStruct
    proj, fhi, flo, whi, wlo, thi, tlo = pl.pallas_call(
        forward_kernel,
        out_shape=[
            sds((3, NX, NY), F32), sds((NX, NX), BF), sds((NX, NX), BF),
            sds((NY, NY), BF), sds((NY, NY), BF), sds((NY, NY), BF), sds((NY, NY), BF),
        ],
        in_specs=[hbm, vmem, hbm, vmem, vmem, vmem],
        out_specs=[vmem] * 7,
        scratch_shapes=[
            pltpu.VMEM((768, NZ), BF),
            pltpu.VMEM((CHUNKS, NZ, 128), BF),
            pltpu.VMEM((CHUNKS, 768, 128), BF),
            pltpu.VMEM((CHUNKS, 16, 48, 128), BF),
            pltpu.VMEM((CHUNKS, 48, 16, 128), BF),
            pltpu.VMEM((CHUNKS, 3, 256, 128), BF),
            pltpu.VMEM((768, 768), BF),
            pltpu.VMEM((NX, NX), F32),
            pltpu.VMEM((2, NX, 256), BF),
            pltpu.VMEM((2, NX, 256), BF),
            pltpu.SemaphoreType.DMA,
            pltpu.SemaphoreType.DMA((CHUNKS,)),
            pltpu.SemaphoreType.DMA((CHUNKS,)),
            pltpu.SemaphoreType.DMA((CHUNKS,)),
            pltpu.SemaphoreType.DMA((CHUNKS,)),
            pltpu.SemaphoreType.DMA((CHUNKS,)),
            pltpu.SemaphoreType.DMA((CHUNKS,)),
            pltpu.SemaphoreType.DMA((3,)),
            pltpu.SemaphoreType.DMA,
        ],
        compiler_params=pltpu.CompilerParams(collective_id=0, has_side_effects=True, vmem_limit_bytes=40 << 20),
    )(blocks, flow_basis, table, flow_mass.reshape(1, NX), wall_basis, wall_mass.reshape(1, NY))

    whole = lambda a: pl.BlockSpec(a.shape, lambda f: (0, 0))
    row_feig, row_weig = flow_eigen.reshape(1, NX), wall_eigen.reshape(1, NY)
    fixed = [fhi, flo, whi, wlo, thi, tlo, row_feig, row_weig]
    plane = pl.BlockSpec((1, NX, NY), lambda f: (f, 0, 0))
    return pl.pallas_call(
        solve_kernel,
        out_shape=sds((3, NX, NY), F32),
        grid=(3,),
        in_specs=[plane] + [whole(a) for a in fixed],
        out_specs=plane,
        compiler_params=pltpu.CompilerParams(vmem_limit_bytes=40 << 20),
    )(proj, *fixed)


def solution(mesh):
    return jax.shard_map(
        local,
        mesh=mesh,
        in_specs=(P("span", "stream", None), P("stream", None), P(), P(), P(), P(), P()),
        out_specs=P(("span", "stream"), None, None),
        check_vma=False,
    )
```

```python
import math

import jax
import jax.numpy as jnp
from jax import lax
from jax.experimental import pallas as pl
from jax.experimental.pallas import tpu as pltpu
from jax.sharding import PartitionSpec as P

NZ, NX, NY = 1536, 512, 256
MESH = pl.DeviceIdType.MESH
VMEM_LIMIT = 63 << 20
BF, F32 = jnp.bfloat16, jnp.float32


def turn_values(quarters, shift):
    nearest = jnp.floor(quarters + 0.5)
    r = (quarters - nearest) * F32(math.pi / 2)
    n = nearest.astype(jnp.int32) + shift
    q = r * r
    cos = 1.0 + q * (-0.5 + q * (F32(1 / 24) + q * (F32(-1 / 720) + q * F32(1 / 40320))))
    sin = r * (1.0 + q * (F32(-1 / 6) + q * (F32(1 / 120) + q * (F32(-1 / 5040) + q * F32(1 / 362880)))))
    odd = (n & 1) == 1
    c = jnp.where(odd, sin, cos)
    s = jnp.where(odd, cos, sin)
    return jnp.where(((n + 1) & 2) == 2, -c, c), jnp.where((n & 2) == 2, -s, s)


def table_rows(i, part, store):
    row = lax.broadcasted_iota(jnp.int32, (128, 128), 0) + 128 * part
    plane = lax.broadcasted_iota(jnp.int32, (128, 128), 1)
    field = 48 * (row & 31) + 24 * ((row >> 5) & 1) + 3 * (row >> 6) + i
    sine = field > NZ // 2
    wavenum = jnp.where(sine, field - NZ // 2, field)
    shift = jnp.where(sine, 1, 0)

    def values(product, shift):
        phase = product.astype(F32)
        phase = phase - F32(NZ) * jnp.floor(phase * F32(1.0 / NZ))
        return turn_values(phase * F32(4.0 / NZ), shift)

    c, s = values(wavenum * plane, shift)
    step_c, step_s = values(wavenum * 128, jnp.zeros_like(shift))
    for a in range(NZ // 128):
        store(a, c.astype(BF))
        c, s = c * step_c - s * step_s, s * step_c + c * step_s


def split(a):
    hi = a.astype(BF)
    return hi, (a - hi.astype(F32)).astype(BF)


def dot(a, b):
    return jnp.dot(a, b, preferred_element_type=F32)


def poisson_kernel(
    div_in, flow_in, fmass_in, wall_in, wmass_in, feig_in, weig_in,
    out_hbm,
    div, flow, fmass, wall, wmass, feig, weig, out, tbl, sbuf, slab, spec, abuf, bbuf, lines, proj, gath, perm,
    fhi, flo, whi, wlo, thi, tlo, fmthi, fmtlo, denom,
    rsem1, rsema, rsemb, ssem1, ssema, ssemb, gsem, gssem, lsem, osem,
):
    s, t = lax.axis_index("span"), lax.axis_index("stream")
    zl, x = s // 4, s % 4
    zh, u = t // 8, t % 8
    z = zh * 8 + zl

    def loop(first, last, body):
        lax.fori_loop(first, last, lambda k, _: (body(k), 0)[1], 0)

    def remote(src, dst, ssem, rsem, device):
        pltpu.make_async_remote_copy(
            src_ref=src, dst_ref=dst, send_sem=ssem, recv_sem=rsem, device_id=device, device_id_type=MESH
        ).start()

    def wait(ref, sem):
        pltpu.make_async_copy(ref, ref, sem).wait()

    def span_peer(k):
        return lax.rem(s // 16 + 1 + k // 16, 2) * 16 + lax.rem(s + k, 16)

    def ring_peer(k):
        step = k // 4
        hops = jnp.where(step % 2 == 0, 8 - step // 2, 9 + step // 2)
        zz = lax.rem(z + hops, 16)
        return zz // 8, lax.rem(zz, 8) * 4 + lax.rem(x + k, 4)

    def group_peer(k):
        return s, zh * 8 + lax.rem(u + k, 8)

    pltpu.make_async_copy(div_in, div, lsem.at[0]).start()
    pltpu.make_async_copy(flow_in, flow, lsem.at[1]).start()
    small = [(fmass_in, fmass), (wall_in, wall), (wmass_in, wmass), (feig_in, feig), (weig_in, weig)]
    for j, (src, dst) in enumerate(small):
        pltpu.make_async_copy(src, dst, lsem.at[2 + j]).start()

    barrier = pltpu.get_barrier_semaphore()

    def greet(peer):
        pl.semaphore_signal(barrier, inc=1, device_id=peer, device_id_type=MESH)

    def greet_ring(k):
        hh, sp = ring_peer(k)
        greet((sp, hh * 8 + u))

    loop(0, 60, greet_ring)
    loop(61, 64, greet_ring)
    loop(1, 8, lambda k: greet(group_peer(k)))

    i0 = lax.broadcasted_iota(jnp.int32, (256, 256), 0)
    i1 = lax.broadcasted_iota(jnp.int32, (256, 256), 1)
    perm[...] = jnp.where(lax.rem(i0, 16) * 16 + i0 // 16 == i1, 1.0, 0.0).astype(BF)

    def gather_nodes(j):
        xp, rows = j // 3, pl.ds(pl.multiple_of(lax.rem(j, 3) * 16, 16), 16)
        block = div[rows, pl.ds(pl.multiple_of(xp * 16, 16), 16), :].reshape(256, NY)
        turned = dot(perm[...], block).astype(BF).reshape(16, 16, NY)
        for b in range(16):
            cols = slice(b % 2 * 128, b % 2 * 128 + 128)
            for yh in range(2):
                sbuf[xp * 16 + b // 2 * 2 + yh, rows, cols] = turned[b, :, yh * 128 : yh * 128 + 128]

    pltpu.make_async_copy(div_in, div, lsem.at[0]).wait()
    loop(0, 6, gather_nodes)
    pl.semaphore_wait(barrier, 70)

    own_planes = slab.at[pl.ds(pl.multiple_of(s * 48, 48), 48), :]

    def send1(k):
        dst = span_peer(k)
        remote(sbuf.at[dst], own_planes, ssem1, rsem1, (dst, t))

    pltpu.make_async_copy(sbuf.at[s], own_planes, rsem1).start()
    loop(0, 16, send1)

    pltpu.make_async_copy(flow_in, flow, lsem.at[1]).wait()
    own_rows = gath.at[pl.ds(pl.multiple_of(t * 32, 32), 32), :]
    pltpu.make_async_copy(flow, own_rows, gsem.at[0]).start()
    remote(flow, own_rows, gssem, gsem.at[1], (lax.rem(s + 16, 32), (1 - zh) * 8 + u))
    loop(1, 8, lambda k: remote(flow, own_rows, gssem, gsem.at[0], group_peer(k)))
    loop(17, 32, send1)

    for j, (src, dst) in enumerate(small):
        pltpu.make_async_copy(src, dst, lsem.at[2 + j]).wait()

    def make_table(j):
        i, part = j // 4, j % 4
        rows = pl.ds(pl.multiple_of(j * 128, 128), 128)

        def store(a, values):
            tbl[rows, a * 128 : (a + 1) * 128] = values

        table_rows(i, part, store)

    loop(0, 12, make_table)

    w = wall[...]
    thi[...], tlo[...] = split(w.T)
    wm = jnp.broadcast_to(wmass[...], (128, NY)).T
    fe = jnp.broadcast_to(feig[...], (128, NX)).T
    for j in range(NY // 128):
        cols = slice(j * 128, (j + 1) * 128)
        whi[:, cols], wlo[:, cols] = split(w[:, cols] * wm)
        denom[:, cols] = fe + weig[:, cols]

    far = (1 - zh) * 8 + u
    far_rows = gath.at[pl.ds(pl.multiple_of(far * 32, 32), 32), :]
    wait(far_rows, gsem.at[1])
    loop(1, 8, lambda k: remote(far_rows, far_rows, gssem, gsem.at[2], group_peer(k)))
    wait(gath.at[pl.ds(0, 256), :], gsem.at[0])
    wait(gath.at[pl.ds(0, 224), :], gsem.at[2])

    fhi[...], flo[...] = split(gath[...])
    fm = jnp.broadcast_to(fmass[...], (128, NX)).T
    node = lax.broadcasted_iota(jnp.int32, (NX, NX), 0)
    spot = lax.broadcasted_iota(jnp.int32, (NX, NX), 1)
    came = (node & 257) + ((node >> 5) & 7) * 2 + ((node >> 1) & 15) * 16
    order = jnp.where(came == spot, 1.0, 0.0).astype(BF)
    for j in range(NX // 128):
        cols = slice(j * 128, (j + 1) * 128)
        hi, lo = split((gath[:, cols] * fm).T)
        fmthi[cols, :] = dot(hi, order).astype(BF)
        fmtlo[cols, :] = dot(lo, order).astype(BF)

    def transform(i):
        for part in range(2):
            rows = pl.ds(pl.multiple_of(i * 512 + part * 256, 256), 256)
            r = dot(tbl[rows, :], slab[...]) * F32(float(NZ) ** -0.5)
            spec[pl.ds(part * 4, 4), i] = r.astype(BF).reshape(4, 64, 256)

    def senda(i):
        def one(k):
            uu = lax.rem(u + k, 8)
            remote(spec.at[uu, i], abuf.at[u, i], ssema, rsema.at[i], group_peer(k))

        pltpu.make_async_copy(spec.at[u, i], abuf.at[u, i], rsema.at[i]).start()
        loop(1, 8, one)

    def turn(i):
        wait(abuf.at[:, i], rsema.at[i])
        for q in range(4):
            rows = pl.ds(q * 16, 16)
            tiles = [abuf[b // 2, i, rows, b % 2 * 128 : b % 2 * 128 + 128] for b in range(16)]
            r = dot(perm[...], jnp.concatenate(tiles, axis=0))
            bbuf[i, rows] = r.astype(BF).reshape(16, 16, 128)

    def sendb(i):
        dst_ref = lines.at[i, s % 2, zh * 16 + s // 2]

        def one(k):
            hh, sp = ring_peer(k)
            remote(bbuf.at[i, hh * 32 + sp], dst_ref, ssemb, rsemb.at[i], (sp, hh * 8 + u))

        loop(0, 60, one)
        pltpu.make_async_copy(bbuf.at[i, zh * 32 + s], dst_ref, rsemb.at[i]).start()
        loop(61, 64, one)

    def solve(i):
        for yh in range(2):
            nodes = lines[i, yh].reshape(NX, 128)
            proj[:, yh * 128 : yh * 128 + 128] = dot(fmthi[...], nodes) + dot(fmtlo[...], nodes)
        f = s * 48 + t * 3 + i
        k = jnp.where(f <= NZ // 2, f, f - NZ // 2).astype(F32) / F32(NZ // 2)
        ahi, alo = split(proj[...])
        coeff = dot(ahi, whi[...]) + (dot(ahi, wlo[...]) + dot(alo, whi[...]))
        shi, slo = split(coeff / (denom[...] + k * k))
        back = dot(fhi[...], shi) + (dot(fhi[...], slo) + dot(flo[...], shi))
        bhi, blo = split(back)
        out[i] = dot(bhi, thi[...]) + (dot(bhi, tlo[...]) + dot(blo, thi[...]))

    wait(slab, rsem1)

    def fields(i):
        transform(i)
        senda(i)

    def share(i):
        turn(i)
        sendb(i)

    def finish(i):
        wait(lines.at[i], rsemb.at[i])
        solve(i)
        pltpu.make_async_copy(out.at[i], out_hbm.at[i], osem).start()

    loop(0, 3, fields)
    loop(0, 3, share)
    loop(0, 3, finish)

    wait(gath.at[pl.ds(0, 480), :], gssem)
    wait(slab.at[pl.ds(0, 31 * 48), :], ssem1)
    wait(spec.at[pl.ds(0, 7)], ssema)
    wait(bbuf.at[:, pl.ds(0, 63)], ssemb)
    pltpu.make_async_copy(out, out_hbm, osem).wait()


def local(divergence, flow_basis, wall_basis, flow_mass, wall_mass, flow_eigen, wall_eigen):
    hbm = pl.BlockSpec(memory_space=pl.ANY)
    dma = pltpu.SemaphoreType.DMA
    return pl.pallas_call(
        poisson_kernel,
        out_shape=jax.ShapeDtypeStruct((3, NX, NY), F32),
        in_specs=[hbm] * 7,
        out_specs=hbm,
        scratch_shapes=[
            pltpu.VMEM((48, 32, NY), BF),
            pltpu.VMEM((32, NX), F32),
            pltpu.VMEM((1, NX), F32),
            pltpu.VMEM((NY, NY), F32),
            pltpu.VMEM((1, NY), F32),
            pltpu.VMEM((1, NX), F32),
            pltpu.VMEM((1, NY), F32),
            pltpu.VMEM((3, NX, NY), F32),
            pltpu.VMEM((NZ, NZ), BF),
            pltpu.VMEM((32, 48, 256), BF),
            pltpu.VMEM((NZ, 256), BF),
            pltpu.VMEM((8, 3, 64, 256), BF),
            pltpu.VMEM((8, 3, 64, 256), BF),
            pltpu.VMEM((3, 64, 16, 128), BF),
            pltpu.VMEM((3, 2, 32, 16, 128), BF),
            pltpu.VMEM((NX, NY), F32),
            pltpu.VMEM((NX, NX), F32),
            pltpu.VMEM((256, 256), BF),
            pltpu.VMEM((NX, NX), BF),
            pltpu.VMEM((NX, NX), BF),
            pltpu.VMEM((NY, NY), BF),
            pltpu.VMEM((NY, NY), BF),
            pltpu.VMEM((NY, NY), BF),
            pltpu.VMEM((NY, NY), BF),
            pltpu.VMEM((NX, NX), BF),
            pltpu.VMEM((NX, NX), BF),
            pltpu.VMEM((NX, NY), F32),
            dma,
            dma((3,)),
            dma((3,)),
            dma,
            dma,
            dma,
            dma((3,)),
            dma,
            dma((7,)),
            dma,
        ],
        compiler_params=pltpu.CompilerParams(collective_id=0, has_side_effects=True, vmem_limit_bytes=VMEM_LIMIT),
    )(
        divergence, flow_basis, flow_mass.reshape(1, NX), wall_basis, wall_mass.reshape(1, NY),
        flow_eigen.reshape(1, NX), wall_eigen.reshape(1, NY),
    )


def solution(mesh):
    return jax.shard_map(
        local,
        mesh=mesh,
        in_specs=(P("span", "stream", None), P("stream", None), P(), P(), P(), P(), P()),
        out_specs=P(("span", "stream"), None, None),
        check_vma=False,
    )
```

```python
import math

import jax
import jax.numpy as jnp
from jax import lax
from jax.experimental import pallas as pl
from jax.experimental.pallas import tpu as pltpu
from jax.sharding import PartitionSpec as P

NZ, NX, NY = 1536, 512, 256
MESH = pl.DeviceIdType.MESH
VMEM_LIMIT = 63 << 20
BF, F32 = jnp.bfloat16, jnp.float32


def turn_values(quarters, shift):
    nearest = jnp.floor(quarters + 0.5)
    r = (quarters - nearest) * F32(math.pi / 2)
    n = nearest.astype(jnp.int32) + shift
    q = r * r
    cos = 1.0 + q * (-0.5 + q * (F32(1 / 24) + q * (F32(-1 / 720) + q * F32(1 / 40320))))
    sin = r * (1.0 + q * (F32(-1 / 6) + q * (F32(1 / 120) + q * (F32(-1 / 5040) + q * F32(1 / 362880)))))
    odd = (n & 1) == 1
    c = jnp.where(odd, sin, cos)
    s = jnp.where(odd, cos, sin)
    return jnp.where(((n + 1) & 2) == 2, -c, c), jnp.where((n & 2) == 2, -s, s)


def table_rows(i, part, store):
    row = lax.broadcasted_iota(jnp.int32, (128, 128), 0) + 128 * part
    plane = lax.broadcasted_iota(jnp.int32, (128, 128), 1)
    owner = 4 * (row & 7) + 2 * ((row >> 4) & 1) + (row >> 8)
    field = 48 * owner + 24 * ((row >> 3) & 1) + 3 * ((row >> 5) & 7) + i
    sine = field > NZ // 2
    wavenum = jnp.where(sine, field - NZ // 2, field)
    shift = jnp.where(sine, 1, 0)

    def values(product, shift):
        phase = product.astype(F32)
        phase = phase - F32(NZ) * jnp.floor(phase * F32(1.0 / NZ))
        return turn_values(phase * F32(4.0 / NZ), shift)

    c, s = values(wavenum * plane, shift)
    step_c, step_s = values(wavenum * 128, jnp.zeros_like(shift))
    for a in range(NZ // 128):
        store(a, c.astype(BF))
        c, s = c * step_c - s * step_s, s * step_c + c * step_s


def split(a):
    hi = a.astype(BF)
    return hi, (a - hi.astype(F32)).astype(BF)


def dot(a, b):
    return jnp.dot(a, b, preferred_element_type=F32)


def poisson_kernel(
    div_in, flow_in, fmass_in, wall_in, wmass_in, feig_in, weig_in,
    out_hbm,
    div, flow, fmass, wall, wmass, feig, weig, out, tbl, sbuf, slab, spec, abuf, bbuf, lines, proj, gath, perm,
    fhi, flo, whi, wlo, thi, tlo, fmthi, fmtlo, denom,
    rsem1, rsema, rsemb, ssem1, ssema, ssemb, gsem, gssem, lsem, osem,
):
    s, t = lax.axis_index("span"), lax.axis_index("stream")
    zl, xhi, xlo = s // 4, (s // 2) % 2, s % 2
    zh, u = t // 8, t % 8
    z = zh * 8 + zl

    def loop(first, last, body):
        lax.fori_loop(first, last, lambda k, _: (body(k), 0)[1], 0)

    def remote(src, dst, ssem, rsem, device):
        pltpu.make_async_remote_copy(
            src_ref=src, dst_ref=dst, send_sem=ssem, recv_sem=rsem, device_id=device, device_id_type=MESH
        ).start()

    def wait(ref, sem):
        pltpu.make_async_copy(ref, ref, sem).wait()

    def span_peer(k):
        return lax.rem(s // 16 + 1 + k // 16, 2) * 16 + lax.rem(s + k, 16)

    def ring_peer(k):
        step = k // 2
        hops = jnp.where(step % 2 == 0, 8 - step // 2, 9 + step // 2)
        zz = lax.rem(z + hops, 16)
        return zz // 8, lax.rem(zz, 8), lax.rem(xhi + k, 2)

    def group_peer(k):
        return s, zh * 8 + lax.rem(u + k, 8)

    def pair_peer(k):
        place = lax.rem(xlo * 8 + u + k, 16)
        return place, (s - xlo + place // 8, zh * 8 + lax.rem(place, 8))

    pltpu.make_async_copy(div_in, div, lsem.at[0]).start()
    pltpu.make_async_copy(flow_in, flow, lsem.at[1]).start()
    small = [(fmass_in, fmass), (wall_in, wall), (wmass_in, wmass), (feig_in, feig), (weig_in, weig)]
    for j, (src, dst) in enumerate(small):
        pltpu.make_async_copy(src, dst, lsem.at[2 + j]).start()

    barrier = pltpu.get_barrier_semaphore()

    def greet(peer):
        pl.semaphore_signal(barrier, inc=1, device_id=peer, device_id_type=MESH)

    loop(0, 16, lambda k: greet((span_peer(k), t)))
    loop(17, 32, lambda k: greet((span_peer(k), t)))
    loop(0, 16, lambda k: greet((2 * k + xlo, (1 - zh) * 8 + u)))
    loop(0, 7, lambda k: greet((s, zh * 8 + lax.rem(u + 1 + k, 8))))
    loop(0, 7, lambda k: greet((s + 1 - 2 * xlo, zh * 8 + lax.rem(u + 1 + k, 8))))

    i0 = lax.broadcasted_iota(jnp.int32, (256, 256), 0)
    i1 = lax.broadcasted_iota(jnp.int32, (256, 256), 1)
    perm[...] = jnp.where(lax.rem(i0, 16) * 16 + i0 // 16 == i1, 1.0, 0.0).astype(BF)

    def gather_nodes(j):
        xp, rows = j // 3, pl.ds(pl.multiple_of(lax.rem(j, 3) * 16, 16), 16)
        block = div[rows, pl.ds(pl.multiple_of(xp * 16, 16), 16), :].reshape(256, NY)
        turned = dot(perm[...], block).astype(BF).reshape(16, 16, NY)
        for c in range(2):
            sbuf[pl.ds(xp * 16, 16), c, rows, :] = turned[:, :, c * 128 : c * 128 + 128]

    pltpu.make_async_copy(div_in, div, lsem.at[0]).wait()
    loop(0, 6, gather_nodes)
    pl.semaphore_wait(barrier, 61)

    own_planes = pl.ds(pl.multiple_of(s * 48, 48), 48)

    def send1(c, first, last):
        def one(k):
            dst = span_peer(k)
            remote(sbuf.at[dst, c], slab.at[c, own_planes], ssem1, rsem1.at[c], (dst, t))

        loop(first, last, one)

    for c in range(2):
        pltpu.make_async_copy(sbuf.at[s, c], slab.at[c, own_planes], rsem1.at[c]).start()
    send1(0, 0, 16)
    send1(0, 17, 32)

    pltpu.make_async_copy(flow_in, flow, lsem.at[1]).wait()
    own_rows = gath.at[pl.ds(pl.multiple_of(t * 32, 32), 32), :]
    pltpu.make_async_copy(flow, own_rows, gsem.at[0]).start()
    remote(flow, own_rows, gssem, gsem.at[1], (lax.rem(s + 16, 32), (1 - zh) * 8 + u))
    loop(1, 8, lambda k: remote(flow, own_rows, gssem, gsem.at[0], group_peer(k)))
    send1(1, 0, 16)
    send1(1, 17, 32)

    for j, (src, dst) in enumerate(small):
        pltpu.make_async_copy(src, dst, lsem.at[2 + j]).wait()

    def make_table(j):
        i, part = j // 4, j % 4
        rows = pl.ds(pl.multiple_of(j * 128, 128), 128)

        def store(a, values):
            tbl[rows, a * 128 : (a + 1) * 128] = values

        table_rows(i, part, store)

    loop(0, 12, make_table)

    w = wall[...]
    thi[...], tlo[...] = split(w.T)
    wm = jnp.broadcast_to(wmass[...], (128, NY)).T
    fe = jnp.broadcast_to(feig[...], (128, NX)).T
    for j in range(NY // 128):
        cols = slice(j * 128, (j + 1) * 128)
        whi[:, cols], wlo[:, cols] = split(w[:, cols] * wm)
        denom[:, cols] = fe + weig[:, cols]

    far = (1 - zh) * 8 + u
    far_rows = gath.at[pl.ds(pl.multiple_of(far * 32, 32), 32), :]
    wait(far_rows, gsem.at[1])
    loop(1, 8, lambda k: remote(far_rows, far_rows, gssem, gsem.at[2], group_peer(k)))
    wait(gath.at[pl.ds(0, 256), :], gsem.at[0])
    wait(gath.at[pl.ds(0, 224), :], gsem.at[2])

    fhi[...], flo[...] = split(gath[...])
    fm = jnp.broadcast_to(fmass[...], (128, NX)).T
    node = lax.broadcasted_iota(jnp.int32, (NX, NX), 0)
    spot = lax.broadcasted_iota(jnp.int32, (NX, NX), 1)
    came = (node & 256) + ((node >> 1) & 15) * 16 + (node & 1) * 8 + ((node >> 5) & 7)
    order = jnp.where(came == spot, 1.0, 0.0).astype(BF)
    for j in range(NX // 128):
        cols = slice(j * 128, (j + 1) * 128)
        hi, lo = split((gath[:, cols] * fm).T)
        fmthi[cols, :] = dot(hi, order).astype(BF)
        fmtlo[cols, :] = dot(lo, order).astype(BF)

    def transform(c, i):
        for part in range(2):
            rows = pl.ds(pl.multiple_of(i * 512 + part * 256, 256), 256)
            r = dot(tbl[rows, :], slab[c]) * F32(float(NZ) ** -0.5)
            spec[c, pl.ds(part * 8, 8), i] = r.astype(BF).reshape(8, 32, 128)

    def senda(c, i):
        here = xlo * 8 + u

        def one(k):
            place, peer = pair_peer(k)
            remote(spec.at[c, place, i], abuf.at[c, here, i], ssema, rsema.at[c, i], peer)

        pltpu.make_async_copy(spec.at[c, here, i], abuf.at[c, here, i], rsema.at[c, i]).start()
        loop(1, 16, one)

    def turn(c, i):
        wait(abuf.at[c, :, i], rsema.at[c, i])
        for q in range(2):
            rows = pl.ds(q * 16, 16)
            r = dot(perm[...], abuf[c, :, i, rows, :].reshape(256, 128))
            bbuf[c, i, rows] = r.astype(BF).reshape(16, 16, 128)

    def sendb(c, i):
        dst_ref = lines.at[c, i, z * 2 + xhi]

        def one(k):
            hh, zz, xx = ring_peer(k)
            remote(
                bbuf.at[c, i, xx * 16 + hh * 8 + zz], dst_ref, ssemb, rsemb.at[c, i],
                (zz * 4 + xx * 2 + xlo, hh * 8 + u),
            )

        loop(0, 30, one)
        pltpu.make_async_copy(bbuf.at[c, i, xhi * 16 + z], dst_ref, rsemb.at[c, i]).start()
        one(31)

    def project(c, i):
        wait(lines.at[c, i], rsemb.at[c, i])
        nodes = lines[c, i].reshape(NX, 128)
        hi, lo = split(dot(fmthi[...], nodes) + dot(fmtlo[...], nodes))
        half = pl.ds(c * 128, 128)
        return dot(hi, whi[half, :]) + (dot(hi, wlo[half, :]) + dot(lo, whi[half, :]))

    def solve(i, coeff):
        f = s * 48 + t * 3 + i
        k = jnp.where(f <= NZ // 2, f, f - NZ // 2).astype(F32) / F32(NZ // 2)
        shi, slo = split(coeff / (denom[...] + k * k))
        back = dot(fhi[...], shi) + (dot(fhi[...], slo) + dot(flo[...], shi))
        bhi, blo = split(back)
        out[i] = dot(bhi, thi[...]) + (dot(bhi, tlo[...]) + dot(blo, thi[...]))

    for c in range(2):
        wait(slab.at[c], rsem1.at[c])

        def fields(i):
            transform(c, i)
            senda(c, i)

        def share(i):
            turn(c, i)
            sendb(c, i)

        loop(0, 3, fields)
        loop(0, 3, share)

    def begin(i):
        proj[i] = project(0, i)

    def finish(i):
        solve(i, proj[i] + project(1, i))
        pltpu.make_async_copy(out.at[i], out_hbm.at[i], osem).start()

    loop(0, 3, begin)
    loop(0, 3, finish)

    wait(gath.at[pl.ds(0, 480), :], gssem)
    wait(slab.at[:, pl.ds(0, 31 * 48), :], ssem1)
    wait(spec.at[:, pl.ds(0, 15)], ssema)
    wait(bbuf.at[:, :, pl.ds(0, 31)], ssemb)
    pltpu.make_async_copy(out, out_hbm, osem).wait()


def local(divergence, flow_basis, wall_basis, flow_mass, wall_mass, flow_eigen, wall_eigen):
    hbm = pl.BlockSpec(memory_space=pl.ANY)
    dma = pltpu.SemaphoreType.DMA
    return pl.pallas_call(
        poisson_kernel,
        out_shape=jax.ShapeDtypeStruct((3, NX, NY), F32),
        in_specs=[hbm] * 7,
        out_specs=hbm,
        scratch_shapes=[
            pltpu.VMEM((48, 32, NY), BF),
            pltpu.VMEM((32, NX), F32),
            pltpu.VMEM((1, NX), F32),
            pltpu.VMEM((NY, NY), F32),
            pltpu.VMEM((1, NY), F32),
            pltpu.VMEM((1, NX), F32),
            pltpu.VMEM((1, NY), F32),
            pltpu.VMEM((3, NX, NY), F32),
            pltpu.VMEM((NZ, NZ), BF),
            pltpu.VMEM((32, 2, 48, 128), BF),
            pltpu.VMEM((2, NZ, 128), BF),
            pltpu.VMEM((2, 16, 3, 32, 128), BF),
            pltpu.VMEM((2, 16, 3, 32, 128), BF),
            pltpu.VMEM((2, 3, 32, 16, 128), BF),
            pltpu.VMEM((2, 3, 32, 16, 128), BF),
            pltpu.VMEM((3, NX, NY), F32),
            pltpu.VMEM((NX, NX), F32),
            pltpu.VMEM((256, 256), BF),
            pltpu.VMEM((NX, NX), BF),
            pltpu.VMEM((NX, NX), BF),
            pltpu.VMEM((NY, NY), BF),
            pltpu.VMEM((NY, NY), BF),
            pltpu.VMEM((NY, NY), BF),
            pltpu.VMEM((NY, NY), BF),
            pltpu.VMEM((NX, NX), BF),
            pltpu.VMEM((NX, NX), BF),
            pltpu.VMEM((NX, NY), F32),
            dma((2,)),
            dma((2, 3)),
            dma((2, 3)),
            dma,
            dma,
            dma,
            dma((3,)),
            dma,
            dma((7,)),
            dma,
        ],
        compiler_params=pltpu.CompilerParams(collective_id=0, has_side_effects=True, vmem_limit_bytes=VMEM_LIMIT),
    )(
        divergence, flow_basis, flow_mass.reshape(1, NX), wall_basis, wall_mass.reshape(1, NY),
        flow_eigen.reshape(1, NX), wall_eigen.reshape(1, NY),
    )


def solution(mesh):
    return jax.shard_map(
        local,
        mesh=mesh,
        in_specs=(P("span", "stream", None), P("stream", None), P(), P(), P(), P(), P()),
        out_specs=P(("span", "stream"), None, None),
        check_vma=False,
    )
```

```python
import math

import jax
import jax.numpy as jnp
from jax import lax
from jax.experimental import pallas as pl
from jax.experimental.pallas import tpu as pltpu
from jax.sharding import PartitionSpec as P

NZ, NX, NY = 1536, 512, 256
MESH = pl.DeviceIdType.MESH
VMEM_LIMIT = 48 << 20
BF, F32 = jnp.bfloat16, jnp.float32


def turn_values(quarters, shift):
    nearest = jnp.floor(quarters + 0.5)
    r = (quarters - nearest) * F32(math.pi / 2)
    n = nearest.astype(jnp.int32) + shift
    q = r * r
    cos = 1.0 + q * (-0.5 + q * (F32(1 / 24) + q * (F32(-1 / 720) + q * F32(1 / 40320))))
    sin = r * (1.0 + q * (F32(-1 / 6) + q * (F32(1 / 120) + q * (F32(-1 / 5040) + q * F32(1 / 362880)))))
    odd = (n & 1) == 1
    c = jnp.where(odd, sin, cos)
    s = jnp.where(odd, cos, sin)
    return jnp.where(((n + 1) & 2) == 2, -c, c), jnp.where((n & 2) == 2, -s, s)


def table_rows(i, part, store):
    row = lax.broadcasted_iota(jnp.int32, (128, 128), 0) + 128 * part
    plane = lax.broadcasted_iota(jnp.int32, (128, 128), 1)
    owner = 4 * (row & 7) + 2 * ((row >> 4) & 1) + (row >> 8)
    field = 48 * owner + 24 * ((row >> 3) & 1) + 3 * ((row >> 5) & 7) + i
    sine = field > NZ // 2
    wavenum = jnp.where(sine, field - NZ // 2, field)
    shift = jnp.where(sine, 1, 0)

    def values(product, shift):
        phase = product.astype(F32)
        phase = phase - F32(NZ) * jnp.floor(phase * F32(1.0 / NZ))
        return turn_values(phase * F32(4.0 / NZ), shift)

    c, s = values(wavenum * plane, shift)
    step_c, step_s = values(wavenum * 128, jnp.zeros_like(shift))
    for a in range(NZ // 128):
        store(a, c.astype(BF))
        c, s = c * step_c - s * step_s, s * step_c + c * step_s


def split(a):
    hi = a.astype(BF)
    return hi, (a - hi.astype(F32)).astype(BF)


def dot(a, b):
    return jnp.dot(a, b, preferred_element_type=F32)


def poisson_kernel(
    div_in, flow_in, fmass_in, wall_in, wmass_in, feig_in, weig_in,
    out,
    div, flow, fmass, wall, wmass, feig, weig, tbl, sbuf, slab, spec, abuf, bbuf, lines, proj, gath, perm,
    fhi, flo, whi, wlo, thi, tlo, fmthi, fmtlo, denom,
    rsem1, rsema, rsemb, ssem1, ssema, ssemb, gsem, gssem, lsem,
):
    s, t = lax.axis_index("span"), lax.axis_index("stream")
    zl, xhi, xlo = s // 4, (s // 2) % 2, s % 2
    zh, u = t // 8, t % 8
    z = zh * 8 + zl

    def loop(first, last, body):
        lax.fori_loop(first, last, lambda k, _: (body(k), 0)[1], 0)

    def remote(src, dst, ssem, rsem, device):
        pltpu.make_async_remote_copy(
            src_ref=src, dst_ref=dst, send_sem=ssem, recv_sem=rsem, device_id=device, device_id_type=MESH
        ).start()

    def wait(ref, sem):
        pltpu.make_async_copy(ref, ref, sem).wait()

    def span_peer(k):
        return lax.rem(s // 16 + 1 + k // 16, 2) * 16 + lax.rem(s + k, 16)

    def ring_peer(k):
        step = k // 2
        hops = jnp.where(step % 2 == 0, 8 - step // 2, 9 + step // 2)
        zz = lax.rem(z + hops, 16)
        return zz // 8, lax.rem(zz, 8), lax.rem(xhi + k, 2)

    def group_peer(k):
        return s, zh * 8 + lax.rem(u + k, 8)

    def pair_peer(k):
        place = lax.rem(xlo * 8 + u + k, 16)
        return place, (s - xlo + place // 8, zh * 8 + lax.rem(place, 8))

    pltpu.make_async_copy(div_in, div, lsem.at[0]).start()
    pltpu.make_async_copy(flow_in, flow, lsem.at[1]).start()
    small = [(fmass_in, fmass), (wall_in, wall), (wmass_in, wmass), (feig_in, feig), (weig_in, weig)]
    for j, (src, dst) in enumerate(small):
        pltpu.make_async_copy(src, dst, lsem.at[2 + j]).start()

    barrier = pltpu.get_barrier_semaphore()

    def greet(peer):
        pl.semaphore_signal(barrier, inc=1, device_id=peer, device_id_type=MESH)

    loop(0, 16, lambda k: greet((span_peer(k), t)))
    loop(17, 32, lambda k: greet((span_peer(k), t)))
    loop(0, 16, lambda k: greet((2 * k + xlo, (1 - zh) * 8 + u)))
    loop(0, 7, lambda k: greet((s, zh * 8 + lax.rem(u + 1 + k, 8))))
    loop(0, 7, lambda k: greet((s + 1 - 2 * xlo, zh * 8 + lax.rem(u + 1 + k, 8))))

    i0 = lax.broadcasted_iota(jnp.int32, (256, 256), 0)
    i1 = lax.broadcasted_iota(jnp.int32, (256, 256), 1)
    perm[...] = jnp.where(lax.rem(i0, 16) * 16 + i0 // 16 == i1, 1.0, 0.0).astype(BF)

    def gather_nodes(j):
        xp, rows = j // 3, pl.ds(pl.multiple_of(lax.rem(j, 3) * 16, 16), 16)
        block = div[rows, pl.ds(pl.multiple_of(xp * 16, 16), 16), :].reshape(256, NY)
        turned = dot(perm[...], block).astype(BF).reshape(16, 16, NY)
        for c in range(2):
            sbuf[pl.ds(xp * 16, 16), c, rows, :] = turned[:, :, c * 128 : c * 128 + 128]

    pltpu.make_async_copy(div_in, div, lsem.at[0]).wait()
    loop(0, 6, gather_nodes)
    pl.semaphore_wait(barrier, 61)

    own_planes = pl.ds(pl.multiple_of(s * 48, 48), 48)

    def send1(c, first, last):
        def one(k):
            dst = span_peer(k)
            remote(sbuf.at[dst, c], slab.at[c, own_planes], ssem1, rsem1.at[c], (dst, t))

        loop(first, last, one)

    for c in range(2):
        pltpu.make_async_copy(sbuf.at[s, c], slab.at[c, own_planes], rsem1.at[c]).start()
    send1(0, 0, 16)
    send1(0, 17, 32)

    pltpu.make_async_copy(flow_in, flow, lsem.at[1]).wait()
    own_rows = gath.at[pl.ds(pl.multiple_of(t * 32, 32), 32), :]
    pltpu.make_async_copy(flow, own_rows, gsem.at[0]).start()
    remote(flow, own_rows, gssem, gsem.at[1], (lax.rem(s + 16, 32), (1 - zh) * 8 + u))
    loop(1, 8, lambda k: remote(flow, own_rows, gssem, gsem.at[0], group_peer(k)))
    send1(1, 0, 16)
    send1(1, 17, 32)

    for j, (src, dst) in enumerate(small):
        pltpu.make_async_copy(src, dst, lsem.at[2 + j]).wait()

    def make_table(j):
        i, part = j // 4, j % 4
        rows = pl.ds(pl.multiple_of(j * 128, 128), 128)

        def store(a, values):
            tbl[rows, a * 128 : (a + 1) * 128] = values

        table_rows(i, part, store)

    loop(0, 12, make_table)

    w = wall[...]
    thi[...], tlo[...] = split(w.T)
    wm = jnp.broadcast_to(wmass[...], (128, NY)).T
    fe = jnp.broadcast_to(feig[...], (128, NX)).T
    for j in range(NY // 128):
        cols = slice(j * 128, (j + 1) * 128)
        whi[:, cols], wlo[:, cols] = split(w[:, cols] * wm)
        denom[:, cols] = fe + weig[:, cols]

    far = (1 - zh) * 8 + u
    far_rows = gath.at[pl.ds(pl.multiple_of(far * 32, 32), 32), :]
    wait(far_rows, gsem.at[1])
    loop(1, 8, lambda k: remote(far_rows, far_rows, gssem, gsem.at[2], group_peer(k)))
    wait(gath.at[pl.ds(0, 256), :], gsem.at[0])
    wait(gath.at[pl.ds(0, 224), :], gsem.at[2])

    fhi[...], flo[...] = split(gath[...])
    fm = jnp.broadcast_to(fmass[...], (128, NX)).T
    node = lax.broadcasted_iota(jnp.int32, (NX, NX), 0)
    spot = lax.broadcasted_iota(jnp.int32, (NX, NX), 1)
    came = (node & 256) + ((node >> 1) & 15) * 16 + (node & 1) * 8 + ((node >> 5) & 7)
    order = jnp.where(came == spot, 1.0, 0.0).astype(BF)
    for j in range(NX // 128):
        cols = slice(j * 128, (j + 1) * 128)
        hi, lo = split((gath[:, cols] * fm).T)
        fmthi[cols, :] = dot(hi, order).astype(BF)
        fmtlo[cols, :] = dot(lo, order).astype(BF)

    def transform(c, i):
        for part in range(2):
            rows = pl.ds(pl.multiple_of(i * 512 + part * 256, 256), 256)
            r = dot(tbl[rows, :], slab[c]) * F32(float(NZ) ** -0.5)
            spec[c, pl.ds(part * 8, 8), i] = r.astype(BF).reshape(8, 32, 128)

    def senda(c, i):
        here = xlo * 8 + u

        def one(k):
            place, peer = pair_peer(k)
            remote(spec.at[c, place, i], abuf.at[c, here, i], ssema, rsema.at[c, i], peer)

        pltpu.make_async_copy(spec.at[c, here, i], abuf.at[c, here, i], rsema.at[c, i]).start()
        loop(1, 16, one)

    def turn(c, i):
        wait(abuf.at[c, :, i], rsema.at[c, i])
        for q in range(2):
            rows = pl.ds(q * 16, 16)
            r = dot(perm[...], abuf[c, :, i, rows, :].reshape(256, 128))
            bbuf[c, i, rows] = r.astype(BF).reshape(16, 16, 128)

    def sendb(c, i):
        dst_ref = lines.at[c, i, z * 2 + xhi]

        def one(k):
            hh, zz, xx = ring_peer(k)
            remote(
                bbuf.at[c, i, xx * 16 + hh * 8 + zz], dst_ref, ssemb, rsemb.at[c, i],
                (zz * 4 + xx * 2 + xlo, hh * 8 + u),
            )

        loop(0, 30, one)
        pltpu.make_async_copy(bbuf.at[c, i, xhi * 16 + z], dst_ref, rsemb.at[c, i]).start()
        one(31)

    def project(c, i):
        wait(lines.at[c, i], rsemb.at[c, i])
        nodes = lines[c, i].reshape(NX, 128)
        hi, lo = split(dot(fmthi[...], nodes) + dot(fmtlo[...], nodes))
        half = pl.ds(c * 128, 128)
        return dot(hi, whi[half, :]) + (dot(hi, wlo[half, :]) + dot(lo, whi[half, :]))

    def solve(i, coeff):
        f = s * 48 + t * 3 + i
        k = jnp.where(f <= NZ // 2, f, f - NZ // 2).astype(F32) / F32(NZ // 2)
        shi, slo = split(coeff / (denom[...] + k * k))
        back = dot(fhi[...], shi) + (dot(fhi[...], slo) + dot(flo[...], shi))
        bhi, blo = split(back)
        out[i] = dot(bhi, thi[...]) + (dot(bhi, tlo[...]) + dot(blo, thi[...]))

    for c in range(2):
        wait(slab.at[c], rsem1.at[c])

        def fields(i):
            transform(c, i)
            senda(c, i)

        def share(i):
            turn(c, i)
            sendb(c, i)

        loop(0, 3, fields)
        loop(0, 3, share)

    def begin(i):
        proj[i] = project(0, i)

    def finish(i):
        solve(i, proj[i] + project(1, i))

    loop(0, 3, begin)
    loop(0, 3, finish)

    wait(gath.at[pl.ds(0, 480), :], gssem)
    wait(slab.at[:, pl.ds(0, 31 * 48), :], ssem1)
    wait(spec.at[:, pl.ds(0, 15)], ssema)
    wait(bbuf.at[:, :, pl.ds(0, 31)], ssemb)


def local(divergence, flow_basis, wall_basis, flow_mass, wall_mass, flow_eigen, wall_eigen):
    hbm = pl.BlockSpec(memory_space=pl.ANY)
    dma = pltpu.SemaphoreType.DMA
    args = [
        divergence, flow_basis, flow_mass.reshape(1, NX), wall_basis, wall_mass.reshape(1, NY),
        flow_eigen.reshape(1, NX), wall_eigen.reshape(1, NY),
    ]
    return pl.pallas_call(
        poisson_kernel,
        out_shape=jax.ShapeDtypeStruct((3, NX, NY), F32),
        in_specs=[hbm] * 7,
        out_specs=pl.BlockSpec(memory_space=pltpu.VMEM),
        scratch_shapes=[
            pltpu.VMEM((48, 32, NY), BF),
            pltpu.VMEM((32, NX), F32),
            pltpu.VMEM((1, NX), F32),
            pltpu.VMEM((NY, NY), F32),
            pltpu.VMEM((1, NY), F32),
            pltpu.VMEM((1, NX), F32),
            pltpu.VMEM((1, NY), F32),
            pltpu.VMEM((NZ, NZ), BF),
            pltpu.VMEM((32, 2, 48, 128), BF),
            pltpu.VMEM((2, NZ, 128), BF),
            pltpu.VMEM((2, 16, 3, 32, 128), BF),
            pltpu.VMEM((2, 16, 3, 32, 128), BF),
            pltpu.VMEM((2, 3, 32, 16, 128), BF),
            pltpu.VMEM((2, 3, 32, 16, 128), BF),
            pltpu.VMEM((3, NX, NY), F32),
            pltpu.VMEM((NX, NX), F32),
            pltpu.VMEM((256, 256), BF),
            pltpu.VMEM((NX, NX), BF),
            pltpu.VMEM((NX, NX), BF),
            pltpu.VMEM((NY, NY), BF),
            pltpu.VMEM((NY, NY), BF),
            pltpu.VMEM((NY, NY), BF),
            pltpu.VMEM((NY, NY), BF),
            pltpu.VMEM((NX, NX), BF),
            pltpu.VMEM((NX, NX), BF),
            pltpu.VMEM((NX, NY), F32),
            dma((2,)),
            dma((2, 3)),
            dma((2, 3)),
            dma,
            dma,
            dma,
            dma((3,)),
            dma,
            dma((7,)),
        ],
        compiler_params=pltpu.CompilerParams(collective_id=0, has_side_effects=True, vmem_limit_bytes=VMEM_LIMIT),
    )(*[pltpu.with_memory_space_constraint(a, pltpu.HBM) for a in args])


def solution(mesh):
    return jax.shard_map(
        local,
        mesh=mesh,
        in_specs=(P("span", "stream", None), P("stream", None), P(), P(), P(), P(), P()),
        out_specs=P(("span", "stream"), None, None),
        check_vma=False,
    )
```

```python
import math

import jax
import jax.numpy as jnp
from jax import lax
from jax.experimental import pallas as pl
from jax.experimental.pallas import tpu as pltpu
from jax.sharding import PartitionSpec as P

NZ, NX, NY = 1536, 512, 256
MESH = pl.DeviceIdType.MESH
VMEM_LIMIT = 48 << 20
BF, F32 = jnp.bfloat16, jnp.float32


def turn_values(quarters, shift):
    nearest = jnp.floor(quarters + 0.5)
    r = (quarters - nearest) * F32(math.pi / 2)
    n = nearest.astype(jnp.int32) + shift
    q = r * r
    cos = 1.0 + q * (-0.5 + q * (F32(1 / 24) + q * (F32(-1 / 720) + q * F32(1 / 40320))))
    sin = r * (1.0 + q * (F32(-1 / 6) + q * (F32(1 / 120) + q * (F32(-1 / 5040) + q * F32(1 / 362880)))))
    odd = (n & 1) == 1
    c = jnp.where(odd, sin, cos)
    s = jnp.where(odd, cos, sin)
    return jnp.where(((n + 1) & 2) == 2, -c, c), jnp.where((n & 2) == 2, -s, s)


def table_rows(i, part, store):
    row = lax.broadcasted_iota(jnp.int32, (128, 128), 0) + 128 * part
    plane = lax.broadcasted_iota(jnp.int32, (128, 128), 1)
    owner = 4 * (row & 7) + 2 * ((row >> 4) & 1) + (row >> 8)
    field = 48 * owner + 24 * ((row >> 3) & 1) + 3 * ((row >> 5) & 7) + i
    sine = field > NZ // 2
    wavenum = jnp.where(sine, field - NZ // 2, field)
    shift = jnp.where(sine, 1, 0)

    def values(product, shift):
        phase = product.astype(F32)
        phase = phase - F32(NZ) * jnp.floor(phase * F32(1.0 / NZ))
        return turn_values(phase * F32(4.0 / NZ), shift)

    c, s = values(wavenum * plane, shift)
    step_c, step_s = values(wavenum * 128, jnp.zeros_like(shift))
    for a in range(NZ // 128):
        store(a, c.astype(BF))
        c, s = c * step_c - s * step_s, s * step_c + c * step_s


def split(a):
    hi = a.astype(BF)
    return hi, (a - hi.astype(F32)).astype(BF)


def dot(a, b):
    return jnp.dot(a, b, preferred_element_type=F32)


def poisson_kernel(
    div_in, flow_in, fmass_in, wall_in, wmass_in, feig_in, weig_in,
    out,
    div, flow, fmass, wall, wmass, feig, weig, tbl, sbuf, slab, spec, abuf, bbuf, lines, proj, gath, perm,
    fhi, flo, whi, wlo, thi, tlo, fmthi, fmtlo, denom,
    rsem1, rsema, rsemb, ssem1, ssema, ssemb, gsem, gssem, lsem,
):
    s, t = lax.axis_index("span"), lax.axis_index("stream")
    zl, xhi, xlo = s // 4, (s // 2) % 2, s % 2
    zh, u = t // 8, t % 8
    z = zh * 8 + zl

    def loop(first, last, body):
        lax.fori_loop(first, last, lambda k, _: (body(k), 0)[1], 0)

    def remote(src, dst, ssem, rsem, device):
        pltpu.make_async_remote_copy(
            src_ref=src, dst_ref=dst, send_sem=ssem, recv_sem=rsem, device_id=device, device_id_type=MESH
        ).start()

    def wait(ref, sem):
        pltpu.make_async_copy(ref, ref, sem).wait()

    def span_peer(k):
        return lax.rem(s // 16 + 1 + k // 16, 2) * 16 + lax.rem(s + k, 16)

    def ring_peer(k):
        step = 15 - k // 2
        hops = jnp.where(step % 2 == 0, 8 - step // 2, 9 + step // 2)
        zz = lax.rem(z + hops, 16)
        return zz // 8, lax.rem(zz, 8), lax.rem(xhi + k, 2)

    def group_peer(k):
        return s, zh * 8 + lax.rem(u + k, 8)

    def pair_peer(k):
        place = lax.rem(xlo * 8 + u + k, 16)
        return place, (s - xlo + place // 8, zh * 8 + lax.rem(place, 8))

    pltpu.make_async_copy(div_in, div, lsem.at[0]).start()
    barrier = pltpu.get_barrier_semaphore()

    def greet(peer):
        pl.semaphore_signal(barrier, inc=1, device_id=peer, device_id_type=MESH)

    loop(0, 16, lambda k: greet((span_peer(k), t)))
    loop(17, 32, lambda k: greet((span_peer(k), t)))
    loop(0, 16, lambda k: greet((2 * k + xlo, (1 - zh) * 8 + u)))
    loop(0, 7, lambda k: greet((s, zh * 8 + lax.rem(u + 1 + k, 8))))
    loop(0, 7, lambda k: greet((s + 1 - 2 * xlo, zh * 8 + lax.rem(u + 1 + k, 8))))

    pltpu.make_async_copy(flow_in, flow, lsem.at[1]).start()
    small = [(fmass_in, fmass), (wall_in, wall), (wmass_in, wmass), (feig_in, feig), (weig_in, weig)]
    for j, (src, dst) in enumerate(small):
        pltpu.make_async_copy(src, dst, lsem.at[2 + j]).start()

    i0 = lax.broadcasted_iota(jnp.int32, (256, 256), 0)
    i1 = lax.broadcasted_iota(jnp.int32, (256, 256), 1)
    perm[...] = jnp.where(lax.rem(i0, 16) * 16 + i0 // 16 == i1, 1.0, 0.0).astype(BF)

    def gather_nodes(c, j):
        xp, rows = j // 3, pl.ds(pl.multiple_of(lax.rem(j, 3) * 16, 16), 16)
        block = div[rows, pl.ds(pl.multiple_of(xp * 16, 16), 16), c * 128 : c * 128 + 128].reshape(256, 128)
        sbuf[pl.ds(xp * 16, 16), c, rows, :] = dot(perm[...], block).astype(BF).reshape(16, 16, 128)

    pltpu.make_async_copy(div_in, div, lsem.at[0]).wait()
    loop(0, 6, lambda j: gather_nodes(0, j))
    pl.semaphore_wait(barrier, 61)

    own_planes = pl.ds(pl.multiple_of(s * 48, 48), 48)

    def send1(c, first, last):
        def one(k):
            dst = span_peer(k)
            remote(sbuf.at[dst, c], slab.at[c, own_planes], ssem1, rsem1.at[c], (dst, t))

        loop(first, last, one)

    def keep(c):
        pltpu.make_async_copy(sbuf.at[s, c], slab.at[c, own_planes], rsem1.at[c]).start()

    send1(0, 0, 16)
    send1(0, 17, 32)
    keep(0)
    loop(0, 6, lambda j: gather_nodes(1, j))
    keep(1)

    pltpu.make_async_copy(flow_in, flow, lsem.at[1]).wait()
    own_rows = gath.at[pl.ds(pl.multiple_of(t * 32, 32), 32), :]
    pltpu.make_async_copy(flow, own_rows, gsem.at[0]).start()
    remote(flow, own_rows, gssem, gsem.at[1], (lax.rem(s + 16, 32), (1 - zh) * 8 + u))
    loop(1, 8, lambda k: remote(flow, own_rows, gssem, gsem.at[0], group_peer(k)))
    send1(1, 0, 16)
    send1(1, 17, 32)

    for j, (src, dst) in enumerate(small):
        pltpu.make_async_copy(src, dst, lsem.at[2 + j]).wait()

    def make_table(j):
        i, part = j // 4, j % 4
        rows = pl.ds(pl.multiple_of(j * 128, 128), 128)

        def store(a, values):
            tbl[rows, a * 128 : (a + 1) * 128] = values

        table_rows(i, part, store)

    loop(0, 12, make_table)

    w = wall[...]
    thi[...], tlo[...] = split(w.T)
    wm = jnp.broadcast_to(wmass[...], (128, NY)).T
    fe = jnp.broadcast_to(feig[...], (128, NX)).T
    for j in range(NY // 128):
        cols = slice(j * 128, (j + 1) * 128)
        whi[:, cols], wlo[:, cols] = split(w[:, cols] * wm)
        denom[:, cols] = fe + weig[:, cols]

    far = (1 - zh) * 8 + u
    far_rows = gath.at[pl.ds(pl.multiple_of(far * 32, 32), 32), :]
    wait(far_rows, gsem.at[1])
    loop(1, 8, lambda k: remote(far_rows, far_rows, gssem, gsem.at[2], group_peer(k)))
    wait(gath.at[pl.ds(0, 256), :], gsem.at[0])
    wait(gath.at[pl.ds(0, 224), :], gsem.at[2])

    fhi[...], flo[...] = split(gath[...])
    fm = jnp.broadcast_to(fmass[...], (128, NX)).T
    node = lax.broadcasted_iota(jnp.int32, (NX, NX), 0)
    spot = lax.broadcasted_iota(jnp.int32, (NX, NX), 1)
    came = (node & 256) + ((node >> 1) & 15) * 16 + (node & 1) * 8 + ((node >> 5) & 7)
    order = jnp.where(came == spot, 1.0, 0.0).astype(BF)
    for j in range(NX // 128):
        cols = slice(j * 128, (j + 1) * 128)
        hi, lo = split((gath[:, cols] * fm).T)
        fmthi[cols, :] = dot(hi, order).astype(BF)
        fmtlo[cols, :] = dot(lo, order).astype(BF)

    def transform(c, i):
        for part in range(2):
            rows = pl.ds(pl.multiple_of(i * 512 + part * 256, 256), 256)
            r = dot(tbl[rows, :], slab[c]) * F32(float(NZ) ** -0.5)
            spec[c, pl.ds(part * 8, 8), i] = r.astype(BF).reshape(8, 32, 128)

    def senda(c, i):
        here = xlo * 8 + u

        def one(k):
            place, peer = pair_peer(k)
            remote(spec.at[c, place, i], abuf.at[c, here, i], ssema, rsema.at[c, i], peer)

        pltpu.make_async_copy(spec.at[c, here, i], abuf.at[c, here, i], rsema.at[c, i]).start()
        loop(1, 16, one)

    def turn(c, i):
        wait(abuf.at[c, :, i], rsema.at[c, i])
        for q in range(2):
            rows = pl.ds(q * 16, 16)
            r = dot(perm[...], abuf[c, :, i, rows, :].reshape(256, 128))
            bbuf[c, i, rows] = r.astype(BF).reshape(16, 16, 128)

    def sendb(c, i):
        dst_ref = lines.at[c, i, z * 2 + xhi]

        def one(k):
            hh, zz, xx = ring_peer(k)
            remote(
                bbuf.at[c, i, xx * 16 + hh * 8 + zz], dst_ref, ssemb, rsemb.at[c, i],
                (zz * 4 + xx * 2 + xlo, hh * 8 + u),
            )

        one(1)
        loop(2, 32, one)
        pltpu.make_async_copy(bbuf.at[c, i, xhi * 16 + z], dst_ref, rsemb.at[c, i]).start()

    def project(c, i):
        wait(lines.at[c, i], rsemb.at[c, i])
        nodes = lines[c, i].reshape(NX, 128)
        hi, lo = split(dot(fmthi[...], nodes) + dot(fmtlo[...], nodes))
        half = pl.ds(c * 128, 128)
        return dot(hi, whi[half, :]) + (dot(hi, wlo[half, :]) + dot(lo, whi[half, :]))

    def solve(i, coeff):
        f = s * 48 + t * 3 + i
        k = jnp.where(f <= NZ // 2, f, f - NZ // 2).astype(F32) / F32(NZ // 2)
        shi, slo = split(coeff / (denom[...] + k * k))
        back = dot(fhi[...], shi) + (dot(fhi[...], slo) + dot(flo[...], shi))
        bhi, blo = split(back)
        out[i] = dot(bhi, thi[...]) + (dot(bhi, tlo[...]) + dot(blo, thi[...]))

    for c in range(2):
        wait(slab.at[c], rsem1.at[c])

        def fields(i):
            transform(c, i)
            senda(c, i)

        def share(i):
            turn(c, i)
            sendb(c, i)

        loop(0, 3, fields)
        loop(0, 3, share)

    def begin(i):
        proj[i] = project(0, i)

    def finish(i):
        solve(i, proj[i] + project(1, i))

    loop(0, 3, begin)
    loop(0, 3, finish)

    wait(gath.at[pl.ds(0, 480), :], gssem)
    wait(slab.at[:, pl.ds(0, 31 * 48), :], ssem1)
    wait(spec.at[:, pl.ds(0, 15)], ssema)
    wait(bbuf.at[:, :, pl.ds(0, 31)], ssemb)


def local(divergence, flow_basis, wall_basis, flow_mass, wall_mass, flow_eigen, wall_eigen):
    hbm = pl.BlockSpec(memory_space=pl.ANY)
    dma = pltpu.SemaphoreType.DMA
    args = [
        divergence, flow_basis, flow_mass.reshape(1, NX), wall_basis, wall_mass.reshape(1, NY),
        flow_eigen.reshape(1, NX), wall_eigen.reshape(1, NY),
    ]
    return pl.pallas_call(
        poisson_kernel,
        out_shape=jax.ShapeDtypeStruct((3, NX, NY), F32),
        in_specs=[hbm] * 7,
        out_specs=pl.BlockSpec(memory_space=pltpu.VMEM),
        scratch_shapes=[
            pltpu.VMEM((48, 32, NY), BF),
            pltpu.VMEM((32, NX), F32),
            pltpu.VMEM((1, NX), F32),
            pltpu.VMEM((NY, NY), F32),
            pltpu.VMEM((1, NY), F32),
            pltpu.VMEM((1, NX), F32),
            pltpu.VMEM((1, NY), F32),
            pltpu.VMEM((NZ, NZ), BF),
            pltpu.VMEM((32, 2, 48, 128), BF),
            pltpu.VMEM((2, NZ, 128), BF),
            pltpu.VMEM((2, 16, 3, 32, 128), BF),
            pltpu.VMEM((2, 16, 3, 32, 128), BF),
            pltpu.VMEM((2, 3, 32, 16, 128), BF),
            pltpu.VMEM((2, 3, 32, 16, 128), BF),
            pltpu.VMEM((3, NX, NY), F32),
            pltpu.VMEM((NX, NX), F32),
            pltpu.VMEM((256, 256), BF),
            pltpu.VMEM((NX, NX), BF),
            pltpu.VMEM((NX, NX), BF),
            pltpu.VMEM((NY, NY), BF),
            pltpu.VMEM((NY, NY), BF),
            pltpu.VMEM((NY, NY), BF),
            pltpu.VMEM((NY, NY), BF),
            pltpu.VMEM((NX, NX), BF),
            pltpu.VMEM((NX, NX), BF),
            pltpu.VMEM((NX, NY), F32),
            dma((2,)),
            dma((2, 3)),
            dma((2, 3)),
            dma,
            dma,
            dma,
            dma((3,)),
            dma,
            dma((7,)),
        ],
        compiler_params=pltpu.CompilerParams(collective_id=0, has_side_effects=True, vmem_limit_bytes=VMEM_LIMIT),
    )(*[pltpu.with_memory_space_constraint(a, pltpu.HBM) for a in args])


def solution(mesh):
    return jax.shard_map(
        local,
        mesh=mesh,
        in_specs=(P("span", "stream", None), P("stream", None), P(), P(), P(), P(), P()),
        out_specs=P(("span", "stream"), None, None),
        check_vma=False,
    )
```
